128 devices in a mesh: tm: 16 (over y, x_lo, core), space: 8 (over z, x_hi).
Axes of the slice: x: 4 (x_hi: 2, x_lo: 2; x = x_hi * 2 + x_lo), y: 4, z: 4, core: 2. Of those that a mesh axis runs over, the one named last changes fastest.
Arguments:
- latents: bfloat16 [256, 64, 128, 128], P(None, 'tm', 'space'), may hold values from -6 to 6
- time_taps: bfloat16 [256, 64], P('tm'), may hold values from -2 to 2
- space_taps: float32 [256, 128, 128], P('tm'), may hold values from -1 to 1
- skip_gain: float32 [256], replicated, may hold values from 0.5 to 1.5
Outputs:
- filtered_video: bfloat16 [256, 64, 128, 128], P(None, 'tm', 'space')
The draws below stay inside these ranges and needn't reach their ends.
All inputs are finite; a program needn't handle non-finite values.
Results may differ from the reference program's by a relative error of at most 0.007.
Values may be sent and summed in bfloat16 or wider, within the bound.
No kernel may reach another device: no remote copies, remote signals or barrier semaphores. Data moves between devices by JAX's collectives and lax.ppermute only.
A program may use at most 128 MiB of HBM per device.

```python
import math
import jax
import jax.numpy as jnp
from jax import lax

C = 256
H = 128
W = 128
FRAMES = 64


def draw_time_taps(key, part):
    key = jax.random.fold_in(key, 11)
    rate_key, noise_key = jax.random.split(key)
    spans = jnp.exp(jax.random.uniform(rate_key, (C, 1), jnp.float32, math.log(FRAMES / 4.0), math.log(8.0 * FRAMES)))
    lags = jnp.arange(FRAMES, dtype=jnp.float32)[None, :]
    envelope = jnp.exp(-lags / spans)
    energy = 0.5 * spans * (1.0 - jnp.exp(-2.0 * FRAMES / spans)) + 0.5
    noise = jnp.clip(jax.random.normal(noise_key, (C, FRAMES), jnp.float32), -4.0, 4.0)
    return (envelope * noise / jnp.sqrt(energy)).astype(jnp.bfloat16)


def draw_space_taps(key, part):
    key = jax.random.fold_in(key, 23)
    reach_key, noise_key = jax.random.split(key)
    reach = jnp.exp(jax.random.uniform(reach_key, (C, 1, 1), jnp.float32, math.log(H / 4.0), math.log(2.0 * H)))
    row_pos = jnp.arange(H, dtype=jnp.float32)
    col_pos = jnp.arange(W, dtype=jnp.float32)
    row_dist = jnp.minimum(row_pos, H - row_pos)[None, :, None]
    col_dist = jnp.minimum(col_pos, W - col_pos)[None, None, :]
    radius = jnp.sqrt(row_dist * row_dist + col_dist * col_dist)
    envelope = jnp.exp(-radius / reach)
    energy = jnp.minimum(0.5 * math.pi * reach * reach, float(H * W)) + 1.0
    noise = jnp.clip(jax.random.normal(noise_key, (C, H, W), jnp.float32), -4.0, 4.0)
    return envelope * noise / jnp.sqrt(energy)


def steps_of(stream_key, dims, cuts, smallest, high):
    loudness = 1.0
    for position, shards_of in cuts:
        heights = jax.random.uniform(jax.random.fold_in(jax.random.fold_in(stream_key, 6), position), (shards_of,), jnp.float32, smallest / len(cuts), high / len(cuts))
        loudness = loudness * jnp.repeat(jnp.exp(heights), dims[position] // shards_of).reshape((-1,) + (1,) * (len(dims) - 1 - position))
    return loudness


def centred(own_key, shape, width, bound, cuts=(), kind=jnp.bfloat16):
    drawn = width * jax.random.normal(own_key, shape, jnp.float32)
    if cuts:
        drawn = drawn * steps_of(own_key, shape, cuts, -0.22, 0.18)
    return jnp.clip(drawn, -bound, bound).astype(kind)


def setup_inputs(seed: int = 0) -> dict:
    keys = jax.random.split(jax.random.key(seed), 5)
    latents = centred(keys[0], (C, FRAMES, H, W), 1.0, 6.0, ((1, 16), (2, 8)))
    time_taps = draw_time_taps(jax.random.fold_in(keys[4], 71), 0)
    space_taps = draw_space_taps(jax.random.fold_in(keys[4], 71), 0)
    skip_gain = jnp.clip(jax.random.uniform(keys[3], (C,), jnp.float32, 0.5, 1.5), 0.5, 1.5)
    return {"latents": latents, "time_taps": time_taps, "space_taps": space_taps, "skip_gain": skip_gain}


def reference(latents, time_taps, space_taps, skip_gain):
    frames = latents.shape[1]

    def one_channel(pair_item):
        channel_video, taps, kernel, gain = pair_item
        values = channel_video.astype(jnp.float32)
        time_spec = jnp.fft.rfft(taps.astype(jnp.float32), 2 * frames)
        video_spec = jnp.fft.rfft(values, 2 * frames, axis=0)
        causal = jnp.fft.irfft(video_spec * time_spec[:, None, None], 2 * frames, axis=0)[:frames]
        convolved = lax.optimization_barrier(causal.astype(jnp.bfloat16))
        spectra = jnp.fft.fft2(convolved.astype(jnp.float32)) * jnp.fft.fft2(kernel)
        filtered = lax.optimization_barrier(jnp.real(jnp.fft.ifft2(spectra)).astype(jnp.bfloat16))
        pre_activation = filtered.astype(jnp.float32) + gain * values
        return jax.nn.gelu(pre_activation, approximate=False).astype(jnp.bfloat16)

    return lax.map(one_channel, (latents, time_taps, space_taps, skip_gain))
```

```python
import functools
import math

import jax
import jax.numpy as jnp
import numpy as np
from jax import lax
from jax.experimental import pallas as pl
from jax.experimental.pallas import tpu as pltpu
from jax.sharding import PartitionSpec as P

AXES = ("tm", "space")
BLOCK = 16
GROUPS_PER_STEP = 4

ERF_TANH = (
    0.7978849411010742,
    0.03633308410644531,
    -3.259458389948122e-05,
    -5.530638009076938e-05,
    3.964782081311569e-06,
    -1.322666491887503e-07,
    1.7562715726171518e-09,
)


def dft_tables(length):
    positions = np.arange(length)
    angles = (positions[:, None] * positions[None, :] % length) * (2.0 * math.pi / length)
    cos, sin = np.cos(angles), np.sin(angles)
    forward = np.block([[cos, -sin], [sin, cos]])
    return forward.astype(np.float32), forward.T.copy().astype(np.float32)


def prepare_kernel(picked_ref, kernel_ref, forward_ref, backward_ref, time_ref, spec_ref):
    rows, cols = time_ref.shape[1], time_ref.shape[2]
    frames = picked_ref.shape[2]

    def spread(shape, along):
        wide = lax.broadcasted_iota(jnp.int32, shape, along) // BLOCK
        return (wide == lax.broadcasted_iota(jnp.int32, shape, 1 - along)).astype(jnp.bfloat16)

    tall = jnp.dot(
        spread((rows, BLOCK), 0), picked_ref[0], preferred_element_type=jnp.float32
    ).astype(jnp.bfloat16)
    full = jnp.dot(tall, spread((frames, cols), 1), preferred_element_type=jnp.float32)
    row_of = lax.broadcasted_iota(jnp.int32, (rows, cols), 0) % BLOCK
    col_of = lax.broadcasted_iota(jnp.int32, (rows, cols), 1) % BLOCK
    time_ref[0] = jnp.where(row_of == col_of, full, 0.0).astype(jnp.bfloat16)

    size = kernel_ref.shape[1]
    exact = lax.Precision.HIGHEST
    half = jnp.dot(
        kernel_ref[0], forward_ref[:size, :], precision=exact, preferred_element_type=jnp.float32
    )
    stacked = jnp.concatenate([half[:, :size], half[:, size:]], axis=0)
    spec = jnp.dot(
        backward_ref[...], stacked, precision=exact, preferred_element_type=jnp.float32
    )
    spec_ref[0] = spec * (1.0 / (size * size))


def gelu(pre):
    square = pre * pre
    q = jnp.float32(ERF_TANH[-1])
    for coefficient in ERF_TANH[-2::-1]:
        q = q * square + jnp.float32(coefficient)
    return 0.5 * pre * (1.0 + jnp.tanh(pre * q))


def filter_kernel(x_ref, time_ref, spec_ref, gain_ref, forward_ref, backward_ref, o_ref, conv):
    tm, space = x_ref.shape[0], x_ref.shape[1]
    per_device = x_ref.shape[3]
    frames, size, _ = conv.shape
    block_rows = BLOCK * BLOCK
    blocks = frames // BLOCK
    devices = BLOCK // per_device

    for pair in range(space // 2):
        for block in range(blocks):
            sources = devices * (block + 1)
            sides = [
                x_ref[0:sources, 2 * pair + side, 0].reshape(block_rows * (block + 1), size)
                for side in range(2)
            ]
            summed = jnp.dot(
                time_ref[0, :, (blocks - 1 - block) * block_rows :],
                jnp.concatenate(sides, axis=1),
                preferred_element_type=jnp.float32,
            ).astype(jnp.bfloat16)
            for side in range(2):
                first = (2 * pair + side) * BLOCK
                conv[block * BLOCK : (block + 1) * BLOCK, first : first + BLOCK, :] = summed[
                    :, side * size : (side + 1) * size
                ].reshape(BLOCK, BLOCK, size)

    gain = gain_ref[0, 0, 0]
    forward = forward_ref[...]
    backward = backward_ref[...]
    group_count = GROUPS_PER_STEP
    pair_count = 2 * group_count

    def stack_rows(value):
        parts = [value[p * size : (p + 1) * size] for p in range(pair_count)]
        return jnp.concatenate(
            [
                jnp.concatenate([part[:, :size] for part in parts], axis=1),
                jnp.concatenate([part[:, size:] for part in parts], axis=1),
            ],
            axis=0,
        )

    def stack_cols(value):
        return jnp.concatenate(
            [
                jnp.concatenate(
                    [
                        value[:size, p * size : (p + 1) * size],
                        value[size:, p * size : (p + 1) * size],
                    ],
                    axis=1,
                )
                for p in range(pair_count)
            ],
            axis=0,
        )

    def dot(a, b):
        return jnp.dot(a, b, preferred_element_type=jnp.float32)

    def step(index, carry):
        start = index * (4 * group_count)
        pairs = [
            jnp.concatenate([conv[start + 2 * p], conv[start + 2 * p + 1]], axis=1)
            for p in range(pair_count)
        ]
        cols = dot(jnp.concatenate(pairs, axis=0), forward).astype(jnp.bfloat16)
        spectrum = dot(backward, stack_rows(cols))
        spec_re = jnp.concatenate([spec_ref[0, :size]] * pair_count, axis=1)
        spec_im = jnp.concatenate([spec_ref[0, size:]] * pair_count, axis=1)
        re, im = spectrum[:size], spectrum[size:]
        product = jnp.concatenate(
            [re * spec_re - im * spec_im, re * spec_im + im * spec_re], axis=0
        ).astype(jnp.bfloat16)
        restored = dot(forward, product).astype(jnp.bfloat16)
        result = dot(stack_cols(restored), backward).astype(jnp.bfloat16)
        for group in range(group_count):
            device = index * group_count + group
            for frame in range(per_device):
                p, side = (4 * group + frame) // 2, frame % 2
                filtered = result[p * size : (p + 1) * size, side * size : (side + 1) * size]
                latent = x_ref[device, :, 0, frame].reshape(size, size)
                pre = filtered.astype(jnp.float32) + gain * latent.astype(jnp.float32)
                o_ref[device, :, 0, frame] = gelu(pre).astype(jnp.bfloat16).reshape(
                    space, BLOCK, size
                )
        return carry

    lax.fori_loop(0, tm // group_count, step, 0)


def local(latents, time_taps, space_taps, skip_gain):
    tm, space = lax.axis_size("tm"), lax.axis_size("space")
    channels, per_device, rows, size = latents.shape
    frames = tm * per_device
    own = channels // (tm * space)
    here = lax.axis_index("space") * own

    received = lax.all_to_all(latents, AXES, split_axis=0, concat_axis=0, tiled=True)
    received = received.reshape(tm, space, own, per_device, rows, size)

    taps = lax.dynamic_slice_in_dim(time_taps, here, own, 0)
    kernels = lax.dynamic_slice_in_dim(space_taps, here, own, 0)
    gains = lax.dynamic_slice_in_dim(skip_gain, lax.axis_index("tm") * own * space + here, own, 0)
    lag = (
        (frames - BLOCK)
        + lax.broadcasted_iota(jnp.int32, (frames, BLOCK, frames), 1)
        - lax.broadcasted_iota(jnp.int32, (frames, BLOCK, frames), 2)
    )
    chosen = lag == lax.broadcasted_iota(jnp.int32, (frames, BLOCK, frames), 0)
    picked = jnp.sum(
        jnp.where(chosen[None], taps.astype(jnp.float32)[:, :, None, None], 0.0), axis=1
    ).astype(jnp.bfloat16)

    forward, backward = (jnp.asarray(table) for table in dft_tables(size))
    wide = BLOCK * BLOCK
    time_matrix, spectra = pl.pallas_call(
        prepare_kernel,
        grid=(own,),
        in_specs=[
            pl.BlockSpec((1, BLOCK, frames), lambda k: (k, 0, 0)),
            pl.BlockSpec((1, size, size), lambda k: (k, 0, 0)),
            pl.BlockSpec((2 * size, 2 * size), lambda k: (0, 0)),
            pl.BlockSpec((2 * size, 2 * size), lambda k: (0, 0)),
        ],
        out_specs=[
            pl.BlockSpec((1, wide, frames * BLOCK), lambda k: (k, 0, 0)),
            pl.BlockSpec((1, 2 * size, size), lambda k: (k, 0, 0)),
        ],
        out_shape=[
            jax.ShapeDtypeStruct((own, wide, frames * BLOCK), jnp.bfloat16),
            jax.ShapeDtypeStruct((own, 2 * size, size), jnp.float32),
        ],
        name="prepare",
    )(picked, kernels, forward, backward)

    block = (tm, space, 1, per_device, rows, size)
    filtered = pl.pallas_call(
        filter_kernel,
        grid=(own,),
        in_specs=[
            pl.BlockSpec(block, lambda k: (0, 0, k, 0, 0, 0)),
            pl.BlockSpec((1, wide, frames * BLOCK), lambda k: (k, 0, 0)),
            pl.BlockSpec((1, 2 * size, size), lambda k: (k, 0, 0)),
            pl.BlockSpec((1, 1, 1), lambda k: (k, 0, 0), memory_space=pltpu.SMEM),
            pl.BlockSpec((2 * size, 2 * size), lambda k: (0, 0)),
            pl.BlockSpec((2 * size, 2 * size), lambda k: (0, 0)),
        ],
        out_specs=pl.BlockSpec(block, lambda k: (0, 0, k, 0, 0, 0)),
        out_shape=jax.ShapeDtypeStruct(received.shape, jnp.bfloat16),
        scratch_shapes=[pltpu.VMEM((frames, size, size), jnp.bfloat16)],
        compiler_params=pltpu.CompilerParams(vmem_limit_bytes=48 * 1024 * 1024),
        name="filter",
    )(
        received,
        time_matrix,
        spectra,
        gains.reshape(own, 1, 1),
        forward.astype(jnp.bfloat16),
        backward.astype(jnp.bfloat16),
    )
    return lax.all_to_all(
        filtered.reshape(latents.shape), AXES, split_axis=0, concat_axis=0, tiled=True
    )


def solution(mesh):
    in_specs = (P(None, "tm", "space", None), P("tm", None), P("tm", None, None), P())
    out_specs = P(None, "tm", "space", None)
    return jax.shard_map(local, mesh=mesh, in_specs=in_specs, out_specs=out_specs, check_vma=False)
```

```python
import math

import jax
import jax.numpy as jnp
import numpy as np
from jax import lax
from jax.experimental import pallas as pl
from jax.experimental.pallas import tpu as pltpu
from jax.sharding import PartitionSpec as P

AXES = ("tm", "space")
BLOCK = 16
GROUPS_PER_STEP = 16


def dft_tables(length):
    positions = np.arange(length)
    angles = (positions[:, None] * positions[None, :] % length) * (2.0 * math.pi / length)
    cos, sin = np.cos(angles), np.sin(angles)
    forward = np.block([[cos, -sin], [sin, cos]])
    return forward.astype(np.float32), forward.T.copy().astype(np.float32)


def prepare_kernel(picked_ref, kernel_ref, forward_ref, backward_ref, time_ref, spec_ref):
    rows, cols = time_ref.shape[1], time_ref.shape[2]
    frames = picked_ref.shape[2]

    def spread(shape, along):
        wide = lax.broadcasted_iota(jnp.int32, shape, along) // BLOCK
        return (wide == lax.broadcasted_iota(jnp.int32, shape, 1 - along)).astype(jnp.bfloat16)

    tall = jnp.dot(
        spread((rows, BLOCK), 0), picked_ref[0], preferred_element_type=jnp.float32
    ).astype(jnp.bfloat16)
    full = jnp.dot(tall, spread((frames, cols), 1), preferred_element_type=jnp.float32)
    row_of = lax.broadcasted_iota(jnp.int32, (rows, cols), 0) % BLOCK
    col_of = lax.broadcasted_iota(jnp.int32, (rows, cols), 1) % BLOCK
    time_ref[0] = jnp.where(row_of == col_of, full, 0.0).astype(jnp.bfloat16)

    size = kernel_ref.shape[1]
    exact = lax.Precision.HIGHEST
    half = jnp.dot(
        kernel_ref[0], forward_ref[:size, :], precision=exact, preferred_element_type=jnp.float32
    )
    stacked = jnp.concatenate([half[:, :size], half[:, size:]], axis=0)
    spec = jnp.dot(
        backward_ref[...], stacked, precision=exact, preferred_element_type=jnp.float32
    )
    spec_ref[0] = spec * (1.0 / (size * size))


def gelu(pre):
    return 0.5 * pre * (1.0 + lax.erf(pre * math.sqrt(0.5)))


def filter_kernel(x_ref, time_ref, spec_ref, gain_ref, forward_ref, backward_ref, o_ref, conv):
    tm, space = x_ref.shape[0], x_ref.shape[1]
    per_device = x_ref.shape[3]
    frames, size, _ = conv.shape
    block_rows = BLOCK * BLOCK
    blocks = frames // BLOCK
    devices = BLOCK // per_device

    for pair in range(space // 2):
        for block in range(blocks):
            sources = devices * (block + 1)
            sides = [
                x_ref[0:sources, 2 * pair + side, 0].reshape(block_rows * (block + 1), size)
                for side in range(2)
            ]
            summed = jnp.dot(
                time_ref[0, :, (blocks - 1 - block) * block_rows :],
                jnp.concatenate(sides, axis=1),
                preferred_element_type=jnp.float32,
            ).astype(jnp.bfloat16)
            for side in range(2):
                first = (2 * pair + side) * BLOCK
                conv[block * BLOCK : (block + 1) * BLOCK, first : first + BLOCK, :] = summed[
                    :, side * size : (side + 1) * size
                ].reshape(BLOCK, BLOCK, size)

    gain = gain_ref[0, 0, 0]
    forward = forward_ref[...]
    backward = backward_ref[...]
    group_count = GROUPS_PER_STEP
    pair_count = 2 * group_count

    def stack_rows(value):
        parts = [value[p * size : (p + 1) * size] for p in range(pair_count)]
        return jnp.concatenate(
            [
                jnp.concatenate([part[:, :size] for part in parts], axis=1),
                jnp.concatenate([part[:, size:] for part in parts], axis=1),
            ],
            axis=0,
        )

    def stack_cols(value):
        return jnp.concatenate(
            [
                jnp.concatenate(
                    [
                        value[:size, p * size : (p + 1) * size],
                        value[size:, p * size : (p + 1) * size],
                    ],
                    axis=1,
                )
                for p in range(pair_count)
            ],
            axis=0,
        )

    def dot(a, b):
        return jnp.dot(a, b, preferred_element_type=jnp.float32)

    def step(index, carry):
        start = index * (4 * group_count)
        pairs = [
            jnp.concatenate([conv[start + 2 * p], conv[start + 2 * p + 1]], axis=1)
            for p in range(pair_count)
        ]
        cols = dot(jnp.concatenate(pairs, axis=0), forward).astype(jnp.bfloat16)
        spectrum = dot(backward, stack_rows(cols))
        spec_re = jnp.concatenate([spec_ref[0, :size]] * pair_count, axis=1)
        spec_im = jnp.concatenate([spec_ref[0, size:]] * pair_count, axis=1)
        re, im = spectrum[:size], spectrum[size:]
        product = jnp.concatenate(
            [re * spec_re - im * spec_im, re * spec_im + im * spec_re], axis=0
        ).astype(jnp.bfloat16)
        restored = dot(forward, product).astype(jnp.bfloat16)
        result = dot(stack_cols(restored), backward)
        for group in range(group_count):
            device = index * group_count + group
            for frame in range(per_device):
                p, side = (4 * group + frame) // 2, frame % 2
                filtered = result[p * size : (p + 1) * size, side * size : (side + 1) * size]
                latent = x_ref[device, :, 0, frame].reshape(size, size)
                pre = filtered + gain * latent.astype(jnp.float32)
                o_ref[device, :, 0, frame] = gelu(pre).astype(jnp.bfloat16).reshape(
                    space, BLOCK, size
                )
        return carry

    lax.fori_loop(0, tm // group_count, step, 0)


def local(latents, time_taps, space_taps, skip_gain):
    tm, space = lax.axis_size("tm"), lax.axis_size("space")
    channels, per_device, rows, size = latents.shape
    frames = tm * per_device
    own = channels // (tm * space)
    here = lax.axis_index("space") * own

    received = lax.all_to_all(latents, AXES, split_axis=0, concat_axis=0, tiled=True)
    received = received.reshape(tm, space, own, per_device, rows, size)

    taps = lax.dynamic_slice_in_dim(time_taps, here, own, 0)
    kernels = lax.dynamic_slice_in_dim(space_taps, here, own, 0)
    gains = lax.dynamic_slice_in_dim(skip_gain, lax.axis_index("tm") * own * space + here, own, 0)
    lag = (
        (frames - BLOCK)
        + lax.broadcasted_iota(jnp.int32, (frames, BLOCK, frames), 1)
        - lax.broadcasted_iota(jnp.int32, (frames, BLOCK, frames), 2)
    )
    chosen = lag == lax.broadcasted_iota(jnp.int32, (frames, BLOCK, frames), 0)
    picked = jnp.sum(
        jnp.where(chosen[None], taps.astype(jnp.float32)[:, :, None, None], 0.0), axis=1
    ).astype(jnp.bfloat16)

    forward, backward = (jnp.asarray(table) for table in dft_tables(size))
    wide = BLOCK * BLOCK
    time_matrix, spectra = pl.pallas_call(
        prepare_kernel,
        grid=(own,),
        in_specs=[
            pl.BlockSpec((1, BLOCK, frames), lambda k: (k, 0, 0)),
            pl.BlockSpec((1, size, size), lambda k: (k, 0, 0)),
            pl.BlockSpec((2 * size, 2 * size), lambda k: (0, 0)),
            pl.BlockSpec((2 * size, 2 * size), lambda k: (0, 0)),
        ],
        out_specs=[
            pl.BlockSpec((1, wide, frames * BLOCK), lambda k: (k, 0, 0)),
            pl.BlockSpec((1, 2 * size, size), lambda k: (k, 0, 0)),
        ],
        out_shape=[
            jax.ShapeDtypeStruct((own, wide, frames * BLOCK), jnp.bfloat16),
            jax.ShapeDtypeStruct((own, 2 * size, size), jnp.float32),
        ],
        name="prepare",
    )(picked, kernels, forward, backward)

    block = (tm, space, 1, per_device, rows, size)
    filtered = pl.pallas_call(
        filter_kernel,
        grid=(own,),
        in_specs=[
            pl.BlockSpec(block, lambda k: (0, 0, k, 0, 0, 0)),
            pl.BlockSpec((1, wide, frames * BLOCK), lambda k: (k, 0, 0)),
            pl.BlockSpec((1, 2 * size, size), lambda k: (k, 0, 0)),
            pl.BlockSpec((1, 1, 1), lambda k: (k, 0, 0), memory_space=pltpu.SMEM),
            pl.BlockSpec((2 * size, 2 * size), lambda k: (0, 0)),
            pl.BlockSpec((2 * size, 2 * size), lambda k: (0, 0)),
        ],
        out_specs=pl.BlockSpec(block, lambda k: (0, 0, k, 0, 0, 0)),
        out_shape=jax.ShapeDtypeStruct(received.shape, jnp.bfloat16),
        scratch_shapes=[pltpu.VMEM((frames, size, size), jnp.bfloat16)],
        compiler_params=pltpu.CompilerParams(vmem_limit_bytes=60 * 1024 * 1024),
        name="filter",
    )(
        received,
        time_matrix,
        spectra,
        gains.reshape(own, 1, 1),
        forward.astype(jnp.bfloat16),
        backward.astype(jnp.bfloat16),
    )
    return lax.all_to_all(
        filtered.reshape(latents.shape), AXES, split_axis=0, concat_axis=0, tiled=True
    )


def solution(mesh):
    in_specs = (P(None, "tm", "space", None), P("tm", None), P("tm", None, None), P())
    out_specs = P(None, "tm", "space", None)
    return jax.shard_map(local, mesh=mesh, in_specs=in_specs, out_specs=out_specs, check_vma=False)
```

```python
import math

import jax
import jax.numpy as jnp
import numpy as np
from jax import lax
from jax.experimental import pallas as pl
from jax.experimental.pallas import tpu as pltpu
from jax.sharding import PartitionSpec as P

AXES = ("tm", "space")
TILE = 8
BLOCK = 32
PARTS = 4
VMEM_LIMIT = 56 * 1024 * 1024


def dft_tables(length):
    positions = np.arange(length)
    angles = (positions[:, None] * positions[None, :] % length) * (2.0 * math.pi / length)
    cos, sin = np.cos(angles), np.sin(angles)
    forward = np.block([[cos, -sin], [sin, cos]])
    return forward.astype(np.float32), forward.T.copy().astype(np.float32)


def prepare_kernel(picked_ref, kernel_ref, forward_ref, backward_ref, time_ref, spec_ref):
    rows, cols = time_ref.shape[1], time_ref.shape[2]
    frames = picked_ref.shape[2]

    def spread(shape, along):
        wide = lax.broadcasted_iota(jnp.int32, shape, along) // TILE
        return (wide == lax.broadcasted_iota(jnp.int32, shape, 1 - along)).astype(jnp.bfloat16)

    tall = jnp.dot(
        spread((rows, BLOCK), 0), picked_ref[0], preferred_element_type=jnp.float32
    ).astype(jnp.bfloat16)
    full = jnp.dot(tall, spread((frames, cols), 1), preferred_element_type=jnp.float32)
    row_of = lax.broadcasted_iota(jnp.int32, (rows, cols), 0) % TILE
    col_of = lax.broadcasted_iota(jnp.int32, (rows, cols), 1) % TILE
    time_ref[0] = jnp.where(row_of == col_of, full, 0.0).astype(jnp.bfloat16)

    size = kernel_ref.shape[1]
    exact = lax.Precision.HIGHEST
    half = jnp.dot(
        kernel_ref[0], forward_ref[:size, :], precision=exact, preferred_element_type=jnp.float32
    )
    stacked = jnp.concatenate([half[:, :size], half[:, size:]], axis=0)
    spec = jnp.dot(
        backward_ref[...], stacked, precision=exact, preferred_element_type=jnp.float32
    )
    spec_ref[0] = spec * (math.sqrt(0.5) / (size * size))


def gelu_of_scaled(scaled):
    half = scaled * math.sqrt(0.5)
    return half + half * lax.erf(scaled)


def filter_kernel(
    x_hbm, time_hbm, spec_hbm, gain_ref, tables_hbm, o_ref,
    x_ref, time_ref, spec_ref, tables_ref, conv, result_a, result_b, in_sems,
):
    own, tm, space, per_device, rows, size = x_ref.shape
    frames = tm * per_device
    side_rows = BLOCK * TILE
    blocks = frames // BLOCK
    pieces = space // 2
    pairs = frames // 2
    devices = tm // (2 * PARTS)
    results = (result_a, result_b)

    def arrival(k, piece):
        return pltpu.make_async_copy(
            x_hbm.at[:, pl.ds(2 * piece, 2), k],
            x_ref.at[k, :, pl.ds(2 * piece, 2)],
            in_sems.at[k * pieces + piece],
        )

    def time_arrival(k):
        return pltpu.make_async_copy(
            time_hbm.at[k], time_ref.at[k], in_sems.at[own * pieces + k]
        )

    others = [
        pltpu.make_async_copy(tables_hbm, tables_ref, in_sems.at[own * pieces + own]),
        pltpu.make_async_copy(spec_hbm, spec_ref, in_sems.at[own * pieces + own + 1]),
    ]

    for k in range(own):
        time_arrival(k).start()
        for piece in range(pieces):
            arrival(k, piece).start()
        if k == 0:
            for other in others:
                other.start()

    def dot(a, b):
        return jnp.dot(a, b, preferred_element_type=jnp.float32)

    def over_time(k, piece):
        sides = [
            x_ref[k, :, 2 * piece + side].reshape(frames, rows, size) for side in range(2)
        ]
        halves = [
            jnp.concatenate(
                [
                    side[:, first : first + TILE].reshape(frames * TILE, size)
                    for side in sides
                ],
                axis=1,
            )
            for first in range(0, rows, TILE)
        ]
        for block in range(blocks):
            summed = jnp.concatenate(
                [
                    dot(
                        time_ref[k, :, (blocks - 1 - block) * side_rows :],
                        half[: (block + 1) * side_rows],
                    ).reshape(BLOCK, TILE, 2 * size)
                    for half in halves
                ],
                axis=1,
            ).astype(jnp.bfloat16)
            for side in range(2):
                conv[block * BLOCK : (block + 1) * BLOCK, 2 * piece + side] = summed[
                    :, :, side * size : (side + 1) * size
                ]

    def stack_rows(value):
        parts = [value[p * size : (p + 1) * size] for p in range(pairs)]
        return jnp.concatenate(
            [
                jnp.concatenate([part[:, :size] for part in parts], axis=1),
                jnp.concatenate([part[:, size:] for part in parts], axis=1),
            ],
            axis=0,
        )

    def stack_cols(value):
        return jnp.concatenate(
            [
                jnp.concatenate(
                    [
                        value[:size, p * size : (p + 1) * size],
                        value[size:, p * size : (p + 1) * size],
                    ],
                    axis=1,
                )
                for p in range(pairs)
            ],
            axis=0,
        )

    def over_space(k):
        forward, backward = tables_ref[0], tables_ref[1]
        images = jnp.concatenate(
            [
                jnp.concatenate(
                    [conv[2 * p + side].reshape(size, size) for side in range(2)], axis=1
                )
                for p in range(pairs)
            ],
            axis=0,
        )
        cols = dot(images, forward).astype(jnp.bfloat16)
        spectrum = dot(backward, stack_rows(cols))
        spec_re = jnp.concatenate([spec_ref[k, :size]] * pairs, axis=1)
        spec_im = jnp.concatenate([spec_ref[k, size:]] * pairs, axis=1)
        re, im = spectrum[:size], spectrum[size:]
        product = jnp.concatenate(
            [re * spec_re - im * spec_im, re * spec_im + im * spec_re], axis=0
        ).astype(jnp.bfloat16)
        restored = stack_cols(dot(forward, product).astype(jnp.bfloat16))
        for half in range(2):
            side = pairs // 2 * size
            results[half][...] = dot(restored[half * side : (half + 1) * side], backward)

    def finish(k, half, part):
        gain = gain_ref[k, 0, 0] * math.sqrt(0.5)
        for place in range(part * devices * per_device, (part + 1) * devices * per_device):
            device, frame = place // per_device, place % per_device
            p, side = place // 2, place % 2
            filtered = results[half][p * size : (p + 1) * size, side * size : (side + 1) * size]
            source = half * (tm // 2) + device
            latent = x_ref[k, source, :, frame].reshape(size, size).astype(jnp.float32)
            o_ref[source, :, k, frame] = (
                gelu_of_scaled(filtered + gain * latent)
                .astype(jnp.bfloat16)
                .reshape(space, rows, size)
            )

    def time_all(k):
        time_arrival(k).wait()
        for piece in range(pieces):
            arrival(k, piece).wait()
        for piece in range(pieces):
            over_time(k, piece)

    def finish_half(k, half):
        for part in range(PARTS):
            finish(k, half, part)

    time_all(0)
    for other in others:
        other.wait()
    for k in range(own):
        over_space(k)
        finish_half(k, 0)
        if k + 1 < own:
            time_all(k + 1)
        finish_half(k, 1)


def local(latents, time_taps, space_taps, skip_gain):
    tm, space = lax.axis_size("tm"), lax.axis_size("space")
    channels, per_device, rows, size = latents.shape
    frames = tm * per_device
    own = channels // (tm * space)
    here = lax.axis_index("space") * own

    received = lax.all_to_all(latents, AXES, split_axis=0, concat_axis=0, tiled=True)
    received = received.reshape(tm, space, own, per_device, rows, size)

    taps = lax.dynamic_slice_in_dim(time_taps, here, own, 0)
    kernels = lax.dynamic_slice_in_dim(space_taps, here, own, 0)
    gains = lax.dynamic_slice_in_dim(skip_gain, lax.axis_index("tm") * own * space + here, own, 0)
    lag = (
        (frames - BLOCK)
        + lax.broadcasted_iota(jnp.int32, (frames, BLOCK, frames), 1)
        - lax.broadcasted_iota(jnp.int32, (frames, BLOCK, frames), 2)
    )
    chosen = lag == lax.broadcasted_iota(jnp.int32, (frames, BLOCK, frames), 0)
    picked = jnp.sum(
        jnp.where(chosen[None], taps.astype(jnp.float32)[:, :, None, None], 0.0), axis=1
    ).astype(jnp.bfloat16)

    forward, backward = (jnp.asarray(table) for table in dft_tables(size))
    wide = BLOCK * TILE
    time_matrix, spectra = pl.pallas_call(
        prepare_kernel,
        grid=(own,),
        in_specs=[
            pl.BlockSpec((1, BLOCK, frames), lambda k: (k, 0, 0)),
            pl.BlockSpec((1, size, size), lambda k: (k, 0, 0)),
            pl.BlockSpec((2 * size, 2 * size), lambda k: (0, 0)),
            pl.BlockSpec((2 * size, 2 * size), lambda k: (0, 0)),
        ],
        out_specs=[
            pl.BlockSpec((1, wide, frames * TILE), lambda k: (k, 0, 0)),
            pl.BlockSpec((1, 2 * size, size), lambda k: (k, 0, 0)),
        ],
        out_shape=[
            jax.ShapeDtypeStruct((own, wide, frames * TILE), jnp.bfloat16),
            jax.ShapeDtypeStruct((own, 2 * size, size), jnp.float32),
        ],
        name="prepare",
    )(picked, kernels, forward, backward)

    hbm = pl.BlockSpec(memory_space=pl.ANY)
    half = (frames // 4 * size, 2 * size)
    filtered = pl.pallas_call(
        filter_kernel,
        in_specs=[hbm, hbm, hbm, pl.BlockSpec(memory_space=pltpu.SMEM), hbm],
        out_specs=pl.BlockSpec(memory_space=pltpu.VMEM),
        out_shape=pltpu.VMEM(received.shape, jnp.bfloat16),
        scratch_shapes=[
            pltpu.VMEM((own, tm, space, per_device, rows, size), jnp.bfloat16),
            pltpu.VMEM(time_matrix.shape, jnp.bfloat16),
            pltpu.VMEM(spectra.shape, jnp.float32),
            pltpu.VMEM((2, 2 * size, 2 * size), jnp.bfloat16),
            pltpu.VMEM((frames, space, rows, size), jnp.bfloat16),
            pltpu.VMEM(half, jnp.float32),
            pltpu.VMEM(half, jnp.float32),
            pltpu.SemaphoreType.DMA((own * (space // 2) + own + 2,)),
        ],
        compiler_params=pltpu.CompilerParams(vmem_limit_bytes=VMEM_LIMIT),
        name="filter",
    )(
        received,
        time_matrix,
        spectra,
        gains.reshape(own, 1, 1),
        jnp.stack([forward, backward]).astype(jnp.bfloat16),
    )
    return lax.all_to_all(
        filtered.reshape(latents.shape), AXES, split_axis=0, concat_axis=0, tiled=True
    )


def solution(mesh):
    in_specs = (P(None, "tm", "space", None), P("tm", None), P("tm", None, None), P())
    out_specs = P(None, "tm", "space", None)
    return jax.shard_map(local, mesh=mesh, in_specs=in_specs, out_specs=out_specs, check_vma=False)
```

```python
import math

import jax
import jax.numpy as jnp
import numpy as np
from jax import lax
from jax.experimental import pallas as pl
from jax.experimental.pallas import tpu as pltpu
from jax.sharding import PartitionSpec as P

AXES = ("tm", "space")
TILE = 8
BLOCK = 32
PARTS = 4
VMEM_LIMIT = 32 * 1024 * 1024


def dft_tables(length):
    positions = np.arange(length)
    angles = (positions[:, None] * positions[None, :] % length) * (2.0 * math.pi / length)
    cos, sin = np.cos(angles), np.sin(angles)
    forward = np.block([[cos, -sin], [sin, cos]])
    return forward.astype(np.float32), forward.T.copy().astype(np.float32)


def gelu_of_scaled(scaled):
    half = scaled * math.sqrt(0.5)
    return half + half * lax.erf(scaled)


def filter_kernel(
    x_ref, taps_ref, exact_ref, kernels_ref, gain_hbm, o_ref,
    tables_ref, rest_ref, time_ref, spec_ref, gain_ref, conv, result_a, result_b, gain_sem,
):
    tm, space, own, per_device, rows, size = x_ref.shape
    frames = tm * per_device
    side_rows = BLOCK * TILE
    blocks = frames // BLOCK
    pieces = space // 2
    pairs = frames // 2
    devices = tm // (2 * PARTS)
    results = (result_a, result_b)
    here = lax.axis_index("space") * own
    group = lax.axis_index("tm") * space * own

    gain_copy = pltpu.make_async_copy(gain_hbm, gain_ref, gain_sem)
    gain_copy.start()

    def dot(a, b):
        return jnp.dot(a, b, preferred_element_type=jnp.float32)

    def two_parts(value):
        high = value.astype(jnp.bfloat16)
        return high, (value - high.astype(jnp.float32)).astype(jnp.bfloat16)

    for table in range(2):
        tables_ref[table], rest_ref[table] = two_parts(exact_ref[table])

    def spread(shape, along):
        wide = lax.broadcasted_iota(jnp.int32, shape, along) // TILE
        return (wide == lax.broadcasted_iota(jnp.int32, shape, 1 - along)).astype(jnp.bfloat16)

    def make_time(k):
        taps = taps_ref[...].astype(jnp.float32)
        row = lax.broadcasted_iota(jnp.int32, taps.shape, 0)
        taps = jnp.sum(jnp.where(row == here + k, taps, 0.0), axis=0, keepdims=True)
        shape = (BLOCK, 2 * frames)
        taps = jnp.broadcast_to(jnp.concatenate([taps, jnp.zeros_like(taps)], axis=1), shape)
        lag = (
            (frames - BLOCK)
            + lax.broadcasted_iota(jnp.int32, shape, 0)
            - lax.broadcasted_iota(jnp.int32, shape, 1)
        )
        picked = jnp.take_along_axis(taps, jnp.maximum(lag, 0), axis=1)
        picked = jnp.where(lag >= 0, picked, 0.0)[:, :frames].astype(jnp.bfloat16)
        tall = dot(spread((side_rows, BLOCK), 0), picked).astype(jnp.bfloat16)
        shape = (side_rows, frames * TILE)
        full = dot(tall, spread((frames, frames * TILE), 1))
        row_of = lax.broadcasted_iota(jnp.int32, shape, 0) % TILE
        col_of = lax.broadcasted_iota(jnp.int32, shape, 1) % TILE
        time_ref[k] = jnp.where(row_of == col_of, full, 0.0).astype(jnp.bfloat16)

    def make_spectra():
        high, rest = two_parts(kernels_ref[pl.ds(here, own)].reshape(own * size, size))
        forward = tables_ref[0, :size]
        half = dot(
            jnp.concatenate([high, rest], axis=1), jnp.concatenate([forward, forward], axis=0)
        ) + dot(high, rest_ref[0, :size])
        stacked = jnp.concatenate(
            [
                jnp.concatenate(
                    [half[k * size : (k + 1) * size, part * size : (part + 1) * size] for part in range(2)],
                    axis=0,
                )
                for k in range(own)
            ],
            axis=1,
        )
        high, rest = two_parts(stacked)
        spectra = dot(tables_ref[1], high) + dot(tables_ref[1], rest) + dot(rest_ref[1], high)
        spectra = spectra * (math.sqrt(0.5) / (size * size))
        for k in range(own):
            spec_ref[k] = spectra[:, k * size : (k + 1) * size]

    def over_time(k, piece):
        sides = [
            x_ref[:, 2 * piece + side, k].reshape(frames, rows, size) for side in range(2)
        ]
        halves = [
            jnp.concatenate(
                [
                    side[:, first : first + TILE].reshape(frames * TILE, size)
                    for side in sides
                ],
                axis=1,
            )
            for first in range(0, rows, TILE)
        ]
        for block in range(blocks):
            summed = jnp.concatenate(
                [
                    dot(
                        time_ref[k, :, (blocks - 1 - block) * side_rows :],
                        half[: (block + 1) * side_rows],
                    ).reshape(BLOCK, TILE, 2 * size)
                    for half in halves
                ],
                axis=1,
            ).astype(jnp.bfloat16)
            for side in range(2):
                conv[block * BLOCK : (block + 1) * BLOCK, 2 * piece + side] = summed[
                    :, :, side * size : (side + 1) * size
                ]

    def stack_rows(value):
        parts = [value[p * size : (p + 1) * size] for p in range(pairs)]
        return jnp.concatenate(
            [
                jnp.concatenate([part[:, :size] for part in parts], axis=1),
                jnp.concatenate([part[:, size:] for part in parts], axis=1),
            ],
            axis=0,
        )

    def stack_cols(value):
        return jnp.concatenate(
            [
                jnp.concatenate(
                    [
                        value[:size, p * size : (p + 1) * size],
                        value[size:, p * size : (p + 1) * size],
                    ],
                    axis=1,
                )
                for p in range(pairs)
            ],
            axis=0,
        )

    def over_space(k):
        forward, backward = tables_ref[0], tables_ref[1]
        images = jnp.concatenate(
            [
                jnp.concatenate(
                    [conv[2 * p + side].reshape(size, size) for side in range(2)], axis=1
                )
                for p in range(pairs)
            ],
            axis=0,
        )
        cols = dot(images, forward).astype(jnp.bfloat16)
        spectrum = dot(backward, stack_rows(cols))
        spec_re = jnp.concatenate([spec_ref[k, :size]] * pairs, axis=1)
        spec_im = jnp.concatenate([spec_ref[k, size:]] * pairs, axis=1)
        re, im = spectrum[:size], spectrum[size:]
        product = jnp.concatenate(
            [re * spec_re - im * spec_im, re * spec_im + im * spec_re], axis=0
        ).astype(jnp.bfloat16)
        restored = stack_cols(dot(forward, product).astype(jnp.bfloat16))
        for half in range(2):
            side = pairs // 2 * size
            results[half][...] = dot(restored[half * side : (half + 1) * side], backward)

    def finish(k, half, part):
        gain = gain_ref[group + here + k] * math.sqrt(0.5)
        for place in range(part * devices * per_device, (part + 1) * devices * per_device):
            device, frame = place // per_device, place % per_device
            p, side = place // 2, place % 2
            filtered = results[half][p * size : (p + 1) * size, side * size : (side + 1) * size]
            source = half * (tm // 2) + device
            latent = x_ref[source, :, k, frame].reshape(size, size).astype(jnp.float32)
            o_ref[source, :, k, frame] = (
                gelu_of_scaled(filtered + gain * latent)
                .astype(jnp.bfloat16)
                .reshape(space, rows, size)
            )

    def time_all(k):
        for piece in range(pieces):
            over_time(k, piece)

    def finish_half(k, half):
        for part in range(PARTS):
            finish(k, half, part)

    make_spectra()
    for k in range(own):
        make_time(k)
    time_all(0)
    gain_copy.wait()
    for k in range(own):
        over_space(k)
        finish_half(k, 0)
        if k + 1 < own:
            time_all(k + 1)
        finish_half(k, 1)


def local(latents, time_taps, space_taps, skip_gain):
    tm, space = lax.axis_size("tm"), lax.axis_size("space")
    channels, per_device, rows, size = latents.shape
    frames = tm * per_device
    own = channels // (tm * space)

    received = lax.all_to_all(latents, AXES, split_axis=0, concat_axis=0, tiled=True)
    received = received.reshape(tm, space, own, per_device, rows, size)

    exact = np.stack(dft_tables(size))
    vmem = pl.BlockSpec(memory_space=pltpu.VMEM)
    half = (frames // 4 * size, 2 * size)
    filtered = pl.pallas_call(
        filter_kernel,
        in_specs=[vmem, vmem, vmem, vmem, pl.BlockSpec(memory_space=pl.ANY)],
        out_specs=vmem,
        out_shape=pltpu.VMEM(received.shape, jnp.bfloat16),
        scratch_shapes=[
            pltpu.VMEM(exact.shape, jnp.bfloat16),
            pltpu.VMEM(exact.shape, jnp.bfloat16),
            pltpu.VMEM((own, BLOCK * TILE, frames * TILE), jnp.bfloat16),
            pltpu.VMEM((own, 2 * size, size), jnp.float32),
            pltpu.SMEM(skip_gain.shape, jnp.float32),
            pltpu.VMEM((frames, space, rows, size), jnp.bfloat16),
            pltpu.VMEM(half, jnp.float32),
            pltpu.VMEM(half, jnp.float32),
            pltpu.SemaphoreType.DMA,
        ],
        compiler_params=pltpu.CompilerParams(vmem_limit_bytes=VMEM_LIMIT),
        name="filter",
    )(
        received,
        time_taps,
        jnp.asarray(exact),
        space_taps,
        skip_gain,
    )
    return lax.all_to_all(
        filtered.reshape(latents.shape), AXES, split_axis=0, concat_axis=0, tiled=True
    )


def solution(mesh):
    in_specs = (P(None, "tm", "space", None), P("tm", None), P("tm", None, None), P())
    out_specs = P(None, "tm", "space", None)
    return jax.shard_map(local, mesh=mesh, in_specs=in_specs, out_specs=out_specs, check_vma=False)
```

```python
import math

import jax
import jax.numpy as jnp
import numpy as np
from jax import lax
from jax.experimental import pallas as pl
from jax.experimental.pallas import tpu as pltpu
from jax.sharding import PartitionSpec as P

AXES = ("tm", "space")
TILE = 8
BLOCK = 32
PARTS = 4
VMEM_LIMIT = 32 * 1024 * 1024


def dft_tables(length):
    positions = np.arange(length)
    angles = (positions[:, None] * positions[None, :] % length) * (2.0 * math.pi / length)
    cos, sin = np.cos(angles), np.sin(angles)
    forward = np.block([[cos, -sin], [sin, cos]])
    return forward.astype(np.float32), forward.T.copy().astype(np.float32)


def gelu_of_scaled(scaled):
    half = scaled * math.sqrt(0.5)
    return half + half * lax.erf(scaled)


def filter_kernel(
    x_ref, taps_ref, exact_ref, kernels_ref, gain_hbm, o_ref,
    tables_ref, rest_ref, time_ref, spec_ref, gain_ref, conv, result_a, result_b, gain_sem,
):
    tm, space, own, per_device, rows, size = x_ref.shape
    frames = tm * per_device
    side_rows = BLOCK * TILE
    blocks = frames // BLOCK
    pieces = space // 2
    pairs = frames // 4
    devices = tm // (2 * PARTS)
    results = (result_a, result_b)
    here = lax.axis_index("space") * own
    group = lax.axis_index("tm") * space * own

    gain_copy = pltpu.make_async_copy(gain_hbm, gain_ref, gain_sem)
    gain_copy.start()

    def dot(a, b):
        return jnp.dot(a, b, preferred_element_type=jnp.float32)

    def two_parts(value):
        high = value.astype(jnp.bfloat16)
        return high, (value - high.astype(jnp.float32)).astype(jnp.bfloat16)

    for table in range(2):
        tables_ref[table], rest_ref[table] = two_parts(exact_ref[table])

    def make_time(k):
        taps = taps_ref[...].astype(jnp.float32)
        row = lax.broadcasted_iota(jnp.int32, taps.shape, 0)
        taps = jnp.sum(jnp.where(row == here + k, taps, 0.0), axis=0, keepdims=True)
        shape = (BLOCK, frames * TILE)
        taps = jnp.broadcast_to(jnp.concatenate([taps] * TILE, axis=1), shape)
        lane = lax.broadcasted_iota(jnp.int32, shape, 1)
        lag = (frames - BLOCK) + lax.broadcasted_iota(jnp.int32, shape, 0) - lane // TILE
        parts = []
        for first in range(0, frames * TILE, size):
            lanes = slice(first, first + size)
            parts.append(
                jnp.take_along_axis(taps[:, lanes], jnp.maximum(lag[:, lanes], 0), axis=1)
            )
        picked = jnp.where(lag >= 0, jnp.concatenate(parts, axis=1), 0.0)
        shape = (TILE, frames * TILE)
        same_row = lax.broadcasted_iota(jnp.int32, shape, 0) == (
            lax.broadcasted_iota(jnp.int32, shape, 1) % TILE
        )
        for target in range(0, BLOCK, 2):
            time_ref[k, target * TILE : (target + 2) * TILE] = jnp.concatenate(
                [
                    jnp.where(same_row, jnp.broadcast_to(picked[t : t + 1], shape), 0.0)
                    for t in (target, target + 1)
                ],
                axis=0,
            ).astype(jnp.bfloat16)

    def make_spectra():
        high, rest = two_parts(kernels_ref[pl.ds(here, own)].reshape(own * size, size))
        forward = tables_ref[0, :size]
        half = dot(
            jnp.concatenate([high, rest], axis=1), jnp.concatenate([forward, forward], axis=0)
        ) + dot(high, rest_ref[0, :size])
        stacked = jnp.concatenate(
            [
                jnp.concatenate(
                    [half[k * size : (k + 1) * size, part * size : (part + 1) * size] for part in range(2)],
                    axis=0,
                )
                for k in range(own)
            ],
            axis=1,
        )
        high, rest = two_parts(stacked)
        spectra = dot(tables_ref[1], high) + dot(tables_ref[1], rest) + dot(rest_ref[1], high)
        spectra = spectra * (math.sqrt(0.5) / (size * size))
        for k in range(own):
            spec_ref[k] = spectra[:, k * size : (k + 1) * size]

    def over_time(k, piece):
        sides = [
            x_ref[:, 2 * piece + side, k].reshape(frames, rows, size).astype(jnp.float32)
            for side in range(2)
        ]
        halves = [
            jnp.concatenate(
                [
                    side[:, first : first + TILE].reshape(frames * TILE, size).astype(jnp.bfloat16)
                    for side in sides
                ],
                axis=1,
            )
            for first in range(0, rows, TILE)
        ]
        for block in range(blocks):
            summed = jnp.concatenate(
                [
                    dot(
                        time_ref[k, :, (blocks - 1 - block) * side_rows :],
                        half[: (block + 1) * side_rows],
                    ).reshape(BLOCK, TILE, 2 * size)
                    for half in halves
                ],
                axis=1,
            ).astype(jnp.bfloat16)
            for side in range(2):
                conv[k, block * BLOCK : (block + 1) * BLOCK, 2 * piece + side] = summed[
                    :, :, side * size : (side + 1) * size
                ]

    def stack_rows(value):
        parts = [value[p * size : (p + 1) * size] for p in range(pairs)]
        return jnp.concatenate(
            [
                jnp.concatenate([part[:, :size] for part in parts], axis=1),
                jnp.concatenate([part[:, size:] for part in parts], axis=1),
            ],
            axis=0,
        )

    def stack_cols(value):
        return jnp.concatenate(
            [
                jnp.concatenate(
                    [
                        value[:size, p * size : (p + 1) * size],
                        value[size:, p * size : (p + 1) * size],
                    ],
                    axis=1,
                )
                for p in range(pairs)
            ],
            axis=0,
        )

    def over_space(k, half):
        forward, backward = tables_ref[0], tables_ref[1]
        first = half * pairs
        images = jnp.concatenate(
            [
                jnp.concatenate(
                    [conv[k, 2 * (first + p) + side].reshape(size, size) for side in range(2)], axis=1
                )
                for p in range(pairs)
            ],
            axis=0,
        )
        cols = dot(images, forward).astype(jnp.bfloat16)
        spectrum = dot(backward, stack_rows(cols))
        spec_re = jnp.concatenate([spec_ref[k, :size]] * pairs, axis=1)
        spec_im = jnp.concatenate([spec_ref[k, size:]] * pairs, axis=1)
        re, im = spectrum[:size], spectrum[size:]
        product = jnp.concatenate(
            [re * spec_re - im * spec_im, re * spec_im + im * spec_re], axis=0
        ).astype(jnp.bfloat16)
        restored = stack_cols(dot(forward, product).astype(jnp.bfloat16))
        results[half][...] = dot(restored, backward)

    def finish(k, half, part):
        gain = gain_ref[group + here + k] * math.sqrt(0.5)
        for place in range(part * devices * per_device, (part + 1) * devices * per_device):
            device, frame = place // per_device, place % per_device
            p, side = place // 2, place % 2
            filtered = results[half][p * size : (p + 1) * size, side * size : (side + 1) * size]
            source = half * (tm // 2) + device
            latent = x_ref[source, :, k, frame].reshape(size, size).astype(jnp.float32)
            o_ref[source, :, k, frame] = (
                gelu_of_scaled(filtered + gain * latent)
                .astype(jnp.bfloat16)
                .reshape(space, rows, size)
            )

    def time_all(k):
        for piece in range(pieces):
            over_time(k, piece)

    def finish_half(k, half):
        for part in range(PARTS):
            finish(k, half, part)

    make_spectra()
    for k in range(own):
        make_time(k)
    time_all(0)
    gain_copy.wait()
    for k in range(1, own):
        time_all(k)
    halves = [(k, half) for k in range(own) for half in range(2)]
    over_space(*halves[0])
    for before, after in zip(halves, halves[1:]):
        finish_half(*before)
        over_space(*after)
    finish_half(*halves[-1])


def local(latents, time_taps, space_taps, skip_gain):
    tm, space = lax.axis_size("tm"), lax.axis_size("space")
    channels, per_device, rows, size = latents.shape
    frames = tm * per_device
    own = channels // (tm * space)

    received = lax.all_to_all(latents, AXES, split_axis=0, concat_axis=0, tiled=True)
    received = received.reshape(tm, space, own, per_device, rows, size)

    exact = np.stack(dft_tables(size))
    vmem = pl.BlockSpec(memory_space=pltpu.VMEM)
    half = (frames // 4 * size, 2 * size)
    filtered = pl.pallas_call(
        filter_kernel,
        in_specs=[vmem, vmem, vmem, vmem, pl.BlockSpec(memory_space=pl.ANY)],
        out_specs=vmem,
        out_shape=pltpu.VMEM(received.shape, jnp.bfloat16),
        scratch_shapes=[
            pltpu.VMEM(exact.shape, jnp.bfloat16),
            pltpu.VMEM(exact.shape, jnp.bfloat16),
            pltpu.VMEM((own, BLOCK * TILE, frames * TILE), jnp.bfloat16),
            pltpu.VMEM((own, 2 * size, size), jnp.float32),
            pltpu.SMEM(skip_gain.shape, jnp.float32),
            pltpu.VMEM((own, frames, space, rows, size), jnp.bfloat16),
            pltpu.VMEM(half, jnp.float32),
            pltpu.VMEM(half, jnp.float32),
            pltpu.SemaphoreType.DMA,
        ],
        compiler_params=pltpu.CompilerParams(vmem_limit_bytes=VMEM_LIMIT),
        name="filter",
    )(
        received,
        time_taps,
        jnp.asarray(exact),
        space_taps,
        skip_gain,
    )
    return lax.all_to_all(
        filtered.reshape(latents.shape), AXES, split_axis=0, concat_axis=0, tiled=True
    )


def solution(mesh):
    in_specs = (P(None, "tm", "space", None), P("tm", None), P("tm", None, None), P())
    out_specs = P(None, "tm", "space", None)
    return jax.shard_map(local, mesh=mesh, in_specs=in_specs, out_specs=out_specs, check_vma=False)
```

```python
import math

import jax
import jax.numpy as jnp
import numpy as np
from jax import lax
from jax.experimental import pallas as pl
from jax.experimental.pallas import tpu as pltpu
from jax.sharding import PartitionSpec as P

AXES = ("tm", "space")
TILE = 8
BLOCK = 32
PARTS = 4
TABLE_SCALE = 1.62475
VMEM_LIMIT = 32 * 1024 * 1024


def dft_tables(length):
    positions = np.arange(length)
    angles = (positions[:, None] * positions[None, :] % length) * (2.0 * math.pi / length)
    cos, sin = TABLE_SCALE * np.cos(angles), TABLE_SCALE * np.sin(angles)
    forward = np.block([[cos, -sin], [sin, cos]])
    return forward.astype(np.float32), forward.T.copy().astype(np.float32)


def gelu_of_scaled(scaled):
    half = scaled * math.sqrt(0.5)
    return half + half * lax.erf(scaled)


def filter_kernel(
    x_ref, taps_ref, exact_ref, kernels_ref, gain_hbm, o_ref,
    tables_ref, rest_ref, time_ref, spec_ref, gain_ref, conv, result_a, result_b, gain_sem,
):
    tm, space, own, per_device, rows, size = x_ref.shape
    frames = tm * per_device
    side_rows = BLOCK * TILE
    blocks = frames // BLOCK
    pieces = space // 2
    pairs = frames // 4
    devices = tm // (2 * PARTS)
    results = (result_a, result_b)
    here = lax.axis_index("space") * own
    group = lax.axis_index("tm") * space * own

    gain_copy = pltpu.make_async_copy(gain_hbm, gain_ref, gain_sem)
    gain_copy.start()

    def dot(a, b):
        return jnp.dot(a, b, preferred_element_type=jnp.float32)

    def two_parts(value):
        high = value.astype(jnp.bfloat16)
        return high, (value - high.astype(jnp.float32)).astype(jnp.bfloat16)

    for table in range(2):
        tables_ref[table], rest_ref[table] = two_parts(exact_ref[table])

    def make_time(k):
        taps = taps_ref[...].astype(jnp.float32)
        row = lax.broadcasted_iota(jnp.int32, taps.shape, 0)
        taps = jnp.sum(jnp.where(row == here + k, taps, 0.0), axis=0, keepdims=True)
        shape = (BLOCK, frames * TILE)
        taps = jnp.broadcast_to(jnp.concatenate([taps] * TILE, axis=1), shape)
        lane = lax.broadcasted_iota(jnp.int32, shape, 1)
        lag = (frames - BLOCK) + lax.broadcasted_iota(jnp.int32, shape, 0) - lane // TILE
        parts = []
        for first in range(0, frames * TILE, size):
            lanes = slice(first, first + size)
            parts.append(
                jnp.take_along_axis(taps[:, lanes], jnp.maximum(lag[:, lanes], 0), axis=1)
            )
        picked = jnp.where(lag >= 0, jnp.concatenate(parts, axis=1), 0.0)
        shape = (TILE, frames * TILE)
        same_row = lax.broadcasted_iota(jnp.int32, shape, 0) == (
            lax.broadcasted_iota(jnp.int32, shape, 1) % TILE
        )
        for target in range(0, BLOCK, 2):
            time_ref[k, target * TILE : (target + 2) * TILE] = jnp.concatenate(
                [
                    jnp.where(same_row, jnp.broadcast_to(picked[t : t + 1], shape), 0.0)
                    for t in (target, target + 1)
                ],
                axis=0,
            ).astype(jnp.bfloat16)

    def make_spectra():
        high, rest = two_parts(kernels_ref[pl.ds(here, own)].reshape(own * size, size))
        forward = tables_ref[0, :size]
        half = dot(
            jnp.concatenate([high, rest], axis=1), jnp.concatenate([forward, forward], axis=0)
        ) + dot(high, rest_ref[0, :size])
        stacked = jnp.concatenate(
            [
                jnp.concatenate(
                    [half[k * size : (k + 1) * size, part * size : (part + 1) * size] for part in range(2)],
                    axis=0,
                )
                for k in range(own)
            ],
            axis=1,
        )
        high, rest = two_parts(stacked)
        spectra = dot(tables_ref[1], high) + dot(tables_ref[1], rest) + dot(rest_ref[1], high)
        spectra = spectra * (math.sqrt(0.5) / (size * size * TABLE_SCALE**6))
        for k in range(own):
            spec_ref[k] = spectra[:, k * size : (k + 1) * size]

    def over_time(k, piece):
        sides = [
            x_ref[:, 2 * piece + side, k].reshape(frames, rows, size).astype(jnp.float32)
            for side in range(2)
        ]
        halves = [
            jnp.concatenate(
                [
                    side[:, first : first + TILE].reshape(frames * TILE, size).astype(jnp.bfloat16)
                    for side in sides
                ],
                axis=1,
            )
            for first in range(0, rows, TILE)
        ]
        for block in range(blocks):
            summed = jnp.concatenate(
                [
                    dot(
                        time_ref[k, :, (blocks - 1 - block) * side_rows :],
                        half[: (block + 1) * side_rows],
                    ).reshape(BLOCK, TILE, 2 * size)
                    for half in halves
                ],
                axis=1,
            ).astype(jnp.bfloat16)
            for side in range(2):
                conv[k, block * BLOCK : (block + 1) * BLOCK, 2 * piece + side] = summed[
                    :, :, side * size : (side + 1) * size
                ]

    def stack_rows(value):
        parts = [value[p * size : (p + 1) * size] for p in range(pairs)]
        return jnp.concatenate(
            [
                jnp.concatenate([part[:, :size] for part in parts], axis=1),
                jnp.concatenate([part[:, size:] for part in parts], axis=1),
            ],
            axis=0,
        )

    def stack_cols(value):
        return jnp.concatenate(
            [
                jnp.concatenate(
                    [
                        value[:size, p * size : (p + 1) * size],
                        value[size:, p * size : (p + 1) * size],
                    ],
                    axis=1,
                )
                for p in range(pairs)
            ],
            axis=0,
        )

    def over_space(k, half):
        forward, backward = tables_ref[0], tables_ref[1]
        first = half * pairs
        images = jnp.concatenate(
            [
                jnp.concatenate(
                    [conv[k, 2 * (first + p) + side].reshape(size, size) for side in range(2)], axis=1
                )
                for p in range(pairs)
            ],
            axis=0,
        )
        cols = dot(images, forward).astype(jnp.bfloat16)
        spectrum = dot(backward, stack_rows(cols))
        spec_re = jnp.concatenate([spec_ref[k, :size]] * pairs, axis=1)
        spec_im = jnp.concatenate([spec_ref[k, size:]] * pairs, axis=1)
        re, im = spectrum[:size], spectrum[size:]
        product = jnp.concatenate(
            [re * spec_re - im * spec_im, re * spec_im + im * spec_re], axis=0
        ).astype(jnp.bfloat16)
        restored = stack_cols(dot(forward, product).astype(jnp.bfloat16))
        results[half][...] = dot(restored, backward)

    def finish(k, half, part):
        gain = gain_ref[group + here + k] * math.sqrt(0.5)
        for place in range(part * devices * per_device, (part + 1) * devices * per_device):
            device, frame = place // per_device, place % per_device
            p, side = place // 2, place % 2
            filtered = results[half][p * size : (p + 1) * size, side * size : (side + 1) * size]
            source = half * (tm // 2) + device
            latent = x_ref[source, :, k, frame].reshape(size, size).astype(jnp.float32)
            o_ref[source, :, k, frame] = (
                gelu_of_scaled(filtered + gain * latent)
                .astype(jnp.bfloat16)
                .reshape(space, rows, size)
            )

    def time_all(k):
        for piece in range(pieces):
            over_time(k, piece)

    def finish_half(k, half):
        for part in range(PARTS):
            finish(k, half, part)

    make_spectra()
    for k in range(own):
        make_time(k)
    time_all(0)
    gain_copy.wait()
    for k in range(1, own):
        time_all(k)
    halves = [(k, half) for k in range(own) for half in range(2)]
    over_space(*halves[0])
    for before, after in zip(halves, halves[1:]):
        finish_half(*before)
        over_space(*after)
    finish_half(*halves[-1])


def local(latents, time_taps, space_taps, skip_gain):
    tm, space = lax.axis_size("tm"), lax.axis_size("space")
    channels, per_device, rows, size = latents.shape
    frames = tm * per_device
    own = channels // (tm * space)

    received = lax.all_to_all(latents, AXES, split_axis=0, concat_axis=0, tiled=True)
    received = received.reshape(tm, space, own, per_device, rows, size)

    exact = np.stack(dft_tables(size))
    vmem = pl.BlockSpec(memory_space=pltpu.VMEM)
    half = (frames // 4 * size, 2 * size)
    filtered = pl.pallas_call(
        filter_kernel,
        in_specs=[vmem, vmem, vmem, vmem, pl.BlockSpec(memory_space=pl.ANY)],
        out_specs=vmem,
        out_shape=pltpu.VMEM(received.shape, jnp.bfloat16),
        scratch_shapes=[
            pltpu.VMEM(exact.shape, jnp.bfloat16),
            pltpu.VMEM(exact.shape, jnp.bfloat16),
            pltpu.VMEM((own, BLOCK * TILE, frames * TILE), jnp.bfloat16),
            pltpu.VMEM((own, 2 * size, size), jnp.float32),
            pltpu.SMEM(skip_gain.shape, jnp.float32),
            pltpu.VMEM((own, frames, space, rows, size), jnp.bfloat16),
            pltpu.VMEM(half, jnp.float32),
            pltpu.VMEM(half, jnp.float32),
            pltpu.SemaphoreType.DMA,
        ],
        compiler_params=pltpu.CompilerParams(vmem_limit_bytes=VMEM_LIMIT),
        name="filter",
    )(
        received,
        time_taps,
        jnp.asarray(exact),
        space_taps,
        skip_gain,
    )
    return lax.all_to_all(
        filtered.reshape(latents.shape), AXES, split_axis=0, concat_axis=0, tiled=True
    )


def solution(mesh):
    in_specs = (P(None, "tm", "space", None), P("tm", None), P("tm", None, None), P())
    out_specs = P(None, "tm", "space", None)
    return jax.shard_map(local, mesh=mesh, in_specs=in_specs, out_specs=out_specs, check_vma=False)
```

```python
import math

import jax
import jax.numpy as jnp
import numpy as np
from jax import lax
from jax.experimental import pallas as pl
from jax.experimental.pallas import tpu as pltpu
from jax.sharding import PartitionSpec as P

AXES = ("tm", "space")
TILE = 8
BLOCK = 32
PARTS = 4
TABLE_SCALE = 1.62475
VMEM_LIMIT = 32 * 1024 * 1024


def dft_tables(length):
    positions = np.arange(length)
    angles = (positions[:, None] * positions[None, :] % length) * (2.0 * math.pi / length)
    cos, sin = TABLE_SCALE * np.cos(angles), TABLE_SCALE * np.sin(angles)
    forward = np.block([[cos, -sin], [sin, cos]])
    return forward.astype(np.float32), forward.T.copy().astype(np.float32)


def gelu_of_scaled(scaled):
    scaled = scaled.astype(jnp.bfloat16)
    half = scaled * jnp.bfloat16(math.sqrt(0.5))
    return half + half * lax.erf(scaled)


def filter_kernel(
    x_ref, taps_ref, exact_ref, kernels_ref, gain_hbm, o_ref,
    tables_ref, rest_ref, time_ref, spec_ref, gain_ref, conv, result_a, result_b, gain_sem,
):
    tm, space, own, per_device, rows, size = x_ref.shape
    frames = tm * per_device
    side_rows = BLOCK * TILE
    blocks = frames // BLOCK
    pieces = space // 2
    pairs = frames // 4
    devices = tm // (2 * PARTS)
    results = (result_a, result_b)
    here = lax.axis_index("space") * own
    group = lax.axis_index("tm") * space * own

    gain_copy = pltpu.make_async_copy(gain_hbm, gain_ref, gain_sem)
    gain_copy.start()

    def dot(a, b):
        return jnp.dot(a, b, preferred_element_type=jnp.float32)

    def two_parts(value):
        high = value.astype(jnp.bfloat16)
        return high, (value - high.astype(jnp.float32)).astype(jnp.bfloat16)

    for table in range(2):
        tables_ref[table], rest_ref[table] = two_parts(exact_ref[table])

    def make_time(k):
        taps = taps_ref[...].astype(jnp.float32)
        row = lax.broadcasted_iota(jnp.int32, taps.shape, 0)
        taps = jnp.sum(jnp.where(row == here + k, taps, 0.0), axis=0, keepdims=True)
        shape = (BLOCK, frames * TILE)
        taps = jnp.broadcast_to(jnp.concatenate([taps] * TILE, axis=1), shape)
        lane = lax.broadcasted_iota(jnp.int32, shape, 1)
        lag = (frames - BLOCK) + lax.broadcasted_iota(jnp.int32, shape, 0) - lane // TILE
        parts = []
        for first in range(0, frames * TILE, size):
            lanes = slice(first, first + size)
            parts.append(
                jnp.take_along_axis(taps[:, lanes], jnp.maximum(lag[:, lanes], 0), axis=1)
            )
        picked = jnp.where(lag >= 0, jnp.concatenate(parts, axis=1), 0.0)
        shape = (TILE, frames * TILE)
        same_row = lax.broadcasted_iota(jnp.int32, shape, 0) == (
            lax.broadcasted_iota(jnp.int32, shape, 1) % TILE
        )
        for target in range(0, BLOCK, 2):
            time_ref[k, target * TILE : (target + 2) * TILE] = jnp.concatenate(
                [
                    jnp.where(same_row, jnp.broadcast_to(picked[t : t + 1], shape), 0.0)
                    for t in (target, target + 1)
                ],
                axis=0,
            ).astype(jnp.bfloat16)

    def make_spectra():
        high, rest = two_parts(kernels_ref[pl.ds(here, own)].reshape(own * size, size))
        forward = tables_ref[0, :size]
        half = dot(
            jnp.concatenate([high, rest], axis=1), jnp.concatenate([forward, forward], axis=0)
        ) + dot(high, rest_ref[0, :size])
        stacked = jnp.concatenate(
            [
                jnp.concatenate(
                    [half[k * size : (k + 1) * size, part * size : (part + 1) * size] for part in range(2)],
                    axis=0,
                )
                for k in range(own)
            ],
            axis=1,
        )
        high, rest = two_parts(stacked)
        spectra = dot(tables_ref[1], high) + dot(tables_ref[1], rest) + dot(rest_ref[1], high)
        spectra = spectra * (math.sqrt(0.5) / (size * size * TABLE_SCALE**6))
        for k in range(own):
            spec_ref[k] = spectra[:, k * size : (k + 1) * size]

    def over_time(k, piece):
        sides = [
            x_ref[:, 2 * piece + side, k].reshape(frames, rows, size).astype(jnp.float32)
            for side in range(2)
        ]
        halves = [
            jnp.concatenate(
                [
                    side[:, first : first + TILE].reshape(frames * TILE, size).astype(jnp.bfloat16)
                    for side in sides
                ],
                axis=1,
            )
            for first in range(0, rows, TILE)
        ]
        for block in range(blocks):
            summed = jnp.concatenate(
                [
                    dot(
                        time_ref[k, :, (blocks - 1 - block) * side_rows :],
                        half[: (block + 1) * side_rows],
                    ).reshape(BLOCK, TILE, 2 * size)
                    for half in halves
                ],
                axis=1,
            ).astype(jnp.bfloat16)
            for side in range(2):
                conv[k, block * BLOCK : (block + 1) * BLOCK, 2 * piece + side] = summed[
                    :, :, side * size : (side + 1) * size
                ]

    def stack_rows(value):
        parts = [value[p * size : (p + 1) * size] for p in range(pairs)]
        return jnp.concatenate(
            [
                jnp.concatenate([part[:, :size] for part in parts], axis=1),
                jnp.concatenate([part[:, size:] for part in parts], axis=1),
            ],
            axis=0,
        )

    def stack_cols(value):
        return jnp.concatenate(
            [
                jnp.concatenate(
                    [
                        value[:size, p * size : (p + 1) * size],
                        value[size:, p * size : (p + 1) * size],
                    ],
                    axis=1,
                )
                for p in range(pairs)
            ],
            axis=0,
        )

    def over_space(k, half):
        forward, backward = tables_ref[0], tables_ref[1]
        first = half * pairs
        images = jnp.concatenate(
            [
                jnp.concatenate(
                    [conv[k, 2 * (first + p) + side].reshape(size, size) for side in range(2)], axis=1
                )
                for p in range(pairs)
            ],
            axis=0,
        )
        cols = dot(images, forward).astype(jnp.bfloat16)
        spectrum = dot(backward, stack_rows(cols))
        spec_re = jnp.concatenate([spec_ref[k, :size]] * pairs, axis=1)
        spec_im = jnp.concatenate([spec_ref[k, size:]] * pairs, axis=1)
        re, im = spectrum[:size], spectrum[size:]
        product = jnp.concatenate(
            [re * spec_re - im * spec_im, re * spec_im + im * spec_re], axis=0
        ).astype(jnp.bfloat16)
        restored = stack_cols(dot(forward, product).astype(jnp.bfloat16))
        results[half][...] = dot(restored, backward)

    def finish(k, half, part):
        gain = gain_ref[group + here + k] * math.sqrt(0.5)
        for place in range(part * devices * per_device, (part + 1) * devices * per_device):
            device, frame = place // per_device, place % per_device
            p, side = place // 2, place % 2
            filtered = results[half][p * size : (p + 1) * size, side * size : (side + 1) * size]
            source = half * (tm // 2) + device
            latent = x_ref[source, :, k, frame].reshape(size, size).astype(jnp.float32)
            o_ref[source, :, k, frame] = (
                gelu_of_scaled(filtered + gain * latent)
                .astype(jnp.bfloat16)
                .reshape(space, rows, size)
            )

    def time_all(k):
        for piece in range(pieces):
            over_time(k, piece)

    def finish_half(k, half):
        for part in range(PARTS):
            finish(k, half, part)

    make_spectra()
    for k in range(own):
        make_time(k)
    time_all(0)
    gain_copy.wait()
    for k in range(1, own):
        time_all(k)
    halves = [(k, half) for k in range(own) for half in range(2)]
    over_space(*halves[0])
    for before, after in zip(halves, halves[1:]):
        finish_half(*before)
        over_space(*after)
    finish_half(*halves[-1])


def local(latents, time_taps, space_taps, skip_gain):
    tm, space = lax.axis_size("tm"), lax.axis_size("space")
    channels, per_device, rows, size = latents.shape
    frames = tm * per_device
    own = channels // (tm * space)

    received = lax.all_to_all(latents, AXES, split_axis=0, concat_axis=0, tiled=True)
    received = received.reshape(tm, space, own, per_device, rows, size)

    exact = np.stack(dft_tables(size))
    vmem = pl.BlockSpec(memory_space=pltpu.VMEM)
    half = (frames // 4 * size, 2 * size)
    filtered = pl.pallas_call(
        filter_kernel,
        in_specs=[vmem, vmem, vmem, vmem, pl.BlockSpec(memory_space=pl.ANY)],
        out_specs=vmem,
        out_shape=pltpu.VMEM(received.shape, jnp.bfloat16),
        scratch_shapes=[
            pltpu.VMEM(exact.shape, jnp.bfloat16),
            pltpu.VMEM(exact.shape, jnp.bfloat16),
            pltpu.VMEM((own, BLOCK * TILE, frames * TILE), jnp.bfloat16),
            pltpu.VMEM((own, 2 * size, size), jnp.float32),
            pltpu.SMEM(skip_gain.shape, jnp.float32),
            pltpu.VMEM((own, frames, space, rows, size), jnp.bfloat16),
            pltpu.VMEM(half, jnp.float32),
            pltpu.VMEM(half, jnp.float32),
            pltpu.SemaphoreType.DMA,
        ],
        compiler_params=pltpu.CompilerParams(vmem_limit_bytes=VMEM_LIMIT),
        name="filter",
    )(
        received,
        time_taps,
        jnp.asarray(exact),
        space_taps,
        skip_gain,
    )
    return lax.all_to_all(
        filtered.reshape(latents.shape), AXES, split_axis=0, concat_axis=0, tiled=True
    )


def solution(mesh):
    in_specs = (P(None, "tm", "space", None), P("tm", None), P("tm", None, None), P())
    out_specs = P(None, "tm", "space", None)
    return jax.shard_map(local, mesh=mesh, in_specs=in_specs, out_specs=out_specs, check_vma=False)
```
